32 devices in a mesh: groups: 2 (over y), cache: 4 (over z), blk: 4 (over x, core).
Axes of the slice: x: 2, y: 2, z: 4, core: 2. Of those that a mesh axis runs over, the one named last changes fastest.
Arguments:
- queries: bfloat16 [8, 512, 2048], P(('groups', 'cache'), 'blk'), parts along dimension 0, may hold values from -6 to 6
- kv_new: bfloat16 [8, 512, 1024], P(('groups', 'cache'), 'blk'), parts along dimension 0, may hold values from -6 to 6
- page_pool: bfloat16 [8, 128, 8, 1024], P(('groups', 'cache')), parts along dimension 0, may hold values from -6 to 6
- page_owner: int32 [8, 4, 32, 1], P(('groups', 'cache'), 'blk'), parts along dimension 0, may hold values from 0 to 3; in each aligned block of 32 rows (0 to 31, 32 to 63, ..., all dimensions but the last counted through in order) at most 16 rows name the same one
- page_slot: int32 [8, 4, 32], P(('groups', 'cache'), 'blk'), parts along dimension 0, may hold values from 0 to 127
- prefix_len: int32 [8], P(('groups', 'cache')), parts along dimension 0, may hold values from 1 to 1024, 2048 in all
- suffix_len: int32 [8], P(('groups', 'cache')), parts along dimension 0, may hold values from 1 to 512, 1536 in all
- ssm_in: bfloat16 [8, 512, 2048], P(('groups', 'cache'), 'blk'), parts along dimension 0, may hold values from -6 to 6
- b_in: bfloat16 [8, 512, 128], P(('groups', 'cache'), 'blk'), parts along dimension 0, may hold values from -4 to 4
- c_in: bfloat16 [8, 512, 128], P(('groups', 'cache'), 'blk'), parts along dimension 0, may hold values from -4 to 4
- step_size: float32 [8, 512, 32], P(('groups', 'cache'), 'blk'), parts along dimension 0, may hold values from 0.01 to 0.1
- decay_rate: float32 [32], replicated, may hold values from 0.001953125 to 4
- skip_gain: float32 [32], replicated, may hold values from 0.5 to 1.5
- prior_state: float32 [8, 32, 64, 128], P(('groups', 'cache')), parts along dimension 0, may hold values from -4 to 4
Outputs:
- attn_out: bfloat16 [8, 512, 2048], P(('groups', 'cache'), 'blk'), parts along dimension 0
- ssm_out: bfloat16 [8, 512, 2048], P(('groups', 'cache'), 'blk'), parts along dimension 0
The draws below stay inside these ranges and needn't reach their ends.
There are 2 independent parts, one for each index of `groups`. The reference program is written for one: setup_inputs(seed, part) draws one part's arguments, and reference() takes and returns one part's arrays. A program takes and returns all parts, laid end to end along the dimension named above; an argument that names none is the same for every part. Nothing has to cross between parts.
Inputs may be any that keep to these rules, and one draw needn't show every extreme that they name: `page_owner`: among the 32 pages of one request at one index of blk, no owner is named more than 16 times, a bound that some block reaches. `prefix_len`: the largest is 1024. `suffix_len`: the largest is 512.
All inputs are finite; a program needn't handle non-finite values. No bound on the sum of `prefix_len` or of `suffix_len` on one device may be relied on, other than what follows from the above.
Results may differ from the reference program's by a relative error of at most 0.008.
Values may be sent and summed in bfloat16 or wider, within the bound.
A program may use at most 128 MiB of HBM per device.

```python
import math
import jax
import jax.numpy as jnp
import numpy as np
from jax import lax

QH = 16
KVH = 4
HD = 128
SH = 32
HP = 64
NS = 128
PAGE = 8
SUF_DEV = 128
LIST = 32
REQ = 4
SUF = 512
PREF = 1024
CAP = 16
POOL = 128
N_CACHE = 4
N_BLK = 4


def paired_draw(key):
    query_key = jax.random.fold_in(key, 101)
    keys_key = jax.random.fold_in(key, 102)
    values_key = jax.random.fold_in(key, 103)
    query_shape = (REQ, SUF, QH * HD)
    half_shape = (REQ, SUF, KVH * HD)
    query_rows = jnp.clip(jax.random.normal(query_key, query_shape, jnp.float32), -6.0, 6.0)
    keys_part = jnp.clip(jax.random.normal(keys_key, half_shape, jnp.float32), -6.0, 6.0)
    values_part = jnp.clip(jax.random.normal(values_key, half_shape, jnp.float32), -6.0, 6.0)
    return (query_rows, jnp.concatenate([keys_part, values_part], axis=-1))


def draw_queries(key, part):
    return paired_draw(key)[0].astype(jnp.bfloat16)


def draw_kv_new(key, part):
    return paired_draw(key)[1].astype(jnp.bfloat16)


def place_ends(drawn, stream_key, least, largest):
    place = [jax.random.randint(jax.random.fold_in(stream_key, axis), (), 0, length) for axis, length in enumerate(drawn.shape)]
    main_axis = drawn.shape.index(max(drawn.shape))
    neighbour = place[:main_axis] + [(place[main_axis] + 1) % drawn.shape[main_axis]] + place[main_axis + 1:]
    return drawn.at[tuple(place)].set(least).at[tuple(neighbour)].set(largest)


def shard_levels(own_key, dims, pieces, smallest, largest):
    level, own = 1.0, jax.random.fold_in(own_key, 6)
    for position, blocks in pieces:
        draws = jnp.exp(jax.random.uniform(jax.random.fold_in(own, position), (blocks,), jnp.float32, smallest / len(pieces), largest / len(pieces)))
        level = level * jnp.repeat(draws, dims[position] // blocks).reshape([-1 if axis == position else 1 for axis in range(len(dims))])
    return level


def split_up(count, total, reach, lean):
    loads = [(1 << 20) // math.isqrt(grade ** lean) + 1 for grade in range(2, count + 1)]
    surplus, given = total - reach - (count - 1), [1] * (count - 1)
    while surplus > 0:
        candidates = [i for i in range(count - 1) if given[i] < reach]
        pool, budget = sum([loads[i] for i in candidates]), surplus
        for i in candidates:
            addition = min(reach - given[i], max(1, budget * loads[i] // pool), surplus)
            given[i] = given[i] + addition
            surplus = surplus - addition
    return np.array([reach] + given)


def ragged_sizes(own_key, count, total, reach, slope):
    if count == 2:
        one = jax.random.randint(own_key, (), max(1, total - reach), min(reach, total - 1) + 1)
        return jnp.stack([one, total - one])
    tallies = jnp.asarray(split_up(count, total, reach, slope), jnp.int32)
    couples = (count - 1) // 2
    donor, receiver = tallies[1:1 + 2 * couples:2], tallies[2:2 + 2 * couples:2]
    margin = jnp.minimum(donor - 1, reach - receiver)
    shifted = jax.random.randint(jax.random.fold_in(own_key, 1), (couples,), 0, 1 << 20) % (margin + 1)
    tallies = tallies.at[1:1 + 2 * couples:2].set(donor - shifted).at[2:2 + 2 * couples:2].set(receiver + shifted)
    return tallies[jax.random.permutation(jax.random.fold_in(own_key, 2), count)]


def shared_out(stream_key, own, number, rows, number_of, top, reach, slope):
    order = jax.random.permutation(stream_key, number_of)
    crowded, ordinary = portions_of(number_of, rows * top, reach, slope, True), portions_of(number_of, rows * top, reach, slope, False)
    places = jnp.arange(number_of)

    def named(sizes, turn):
        used = int((sizes > 0).sum())
        fixed = max(1, used // 4)
        moved = fixed + (places - fixed + turn * (used - fixed)) % max(1, number_of - fixed)
        return jnp.zeros((number_of,), jnp.int32).at[order[jnp.where(places < fixed, places, moved)]].set(jnp.asarray(sizes, jnp.int32))

    sizes = jnp.where(number % 4 == 0, named(crowded, number // 4), named(ordinary, number - number // 4 - 1))
    mixed = jax.random.permutation(jax.random.fold_in(own, 3), number_of)
    giver, receiver = mixed[0:number_of // 2 * 2:2], mixed[1:number_of // 2 * 2:2]
    margin = jnp.minimum(sizes[giver] - 1, reach - sizes[receiver]) // 2
    margin = jnp.where((giver == order[0]) | (receiver == order[0]) | (sizes[receiver] == 0), 0, jnp.maximum(margin, 0))
    moved = jax.random.randint(jax.random.fold_in(own, 4), (number_of // 2,), 0, 1 << 20) % (margin + 1)
    sizes = sizes.at[giver].add(-moved).at[receiver].add(moved)
    labels = jnp.searchsorted(jnp.cumsum(sizes), jnp.arange(rows * top), side="right").astype(jnp.int32)
    grid = labels.reshape(top, rows).T
    grid = grid[jax.random.permutation(jax.random.fold_in(own, 1), rows)]
    turn = jax.random.randint(jax.random.fold_in(own, 2), (rows, 1), 0, top)
    return jnp.take_along_axis(grid, (jnp.arange(top)[None, :] + turn) % top, axis=1)


def portions_of(count, total, bound, skew, full):
    portions = [(1 << 20) // math.isqrt(rank ** skew) + 1 for rank in range(1, count + 1)]
    largest = bound if full else min(bound, max(-(-total // count), total * portions[0] // sum(portions)))
    least = 1 if total - largest >= count - 1 else 0
    given, rest = [largest] + [least] * (count - 1), total - largest - least * (count - 1)
    while rest > 0:
        free = [i for i in range(1, count) if given[i] < largest] or [i for i in range(1, count) if given[i] < bound]
        mass, remaining = sum([portions[i] for i in free]), rest
        for i in free:
            extra = min(bound - given[i], max(1, remaining * portions[i] // mass), rest)
            given[i] = given[i] + extra
            rest = rest - extra
    return np.array(given)


def noise(rng, dims, spread, reach, shards=(), held_as=jnp.bfloat16):
    gain = shard_levels(rng, dims, shards, -0.22, 0.18) if shards else 1.0
    values = jax.random.normal(rng, dims, jnp.float32) * spread * gain
    return jnp.minimum(jnp.maximum(values, -reach), reach).astype(held_as)


def setup_inputs(seed: int = 0, part: int = 0) -> dict:
    key_list = jax.random.split(jax.random.key(seed), 15)
    part_splits = jax.random.split(jax.random.fold_in(key_list[14], part), 15)
    queries = draw_queries(jax.random.fold_in(jax.random.fold_in(key_list[14], part), 71), part)
    kv_new = draw_kv_new(jax.random.fold_in(jax.random.fold_in(key_list[14], part), 71), part)
    page_pool = noise(part_splits[2], (N_CACHE, POOL, PAGE, 2 * KVH * HD), 1.0, 6.0, ((0, 4),))
    page_owner_keys = jax.random.split(jax.random.fold_in(part_splits[3], 1), REQ * N_BLK * LIST // LIST)
    page_owner_turns = jax.random.permutation(jax.random.fold_in(part_splits[3], 3), REQ * N_BLK * LIST // LIST)
    page_owner = jax.vmap(lambda own, number: shared_out(jax.random.fold_in(part_splits[3], 2), own, number, LIST, N_CACHE, 1, CAP, 2))(page_owner_keys, page_owner_turns).reshape((REQ, N_BLK, LIST, 1))
    page_slot = place_ends(jax.random.randint(part_splits[4], (REQ, N_BLK, LIST), 0, POOL), jax.random.fold_in(part_splits[4], 1), 0, POOL - 1).astype(jnp.int32)
    prefix_len = ragged_sizes(part_splits[5], REQ, REQ * PREF // 2, PREF, 2).astype(jnp.int32)
    suffix_len = ragged_sizes(part_splits[6], REQ, REQ * SUF * 3 // 4, SUF, 2).astype(jnp.int32)
    ssm_in = noise(part_splits[7], (REQ, SUF, SH * HP), 1.0, 6.0, ((0, 4), (1, 4)))
    b_in = noise(part_splits[8], (REQ, SUF, NS), 0.25, 4.0, ((0, 4), (1, 4)))
    c_in = noise(part_splits[9], (REQ, SUF, NS), 0.25, 4.0, ((0, 4), (1, 4)))
    step_size = jnp.clip(jnp.exp(math.log(0.1) - 2.3025851 * jax.random.uniform(part_splits[10], (REQ, SUF, SH), jnp.float32) ** shard_levels(part_splits[10], (REQ, SUF, SH), ((0, 4), (1, 4)), -0.2, 0.2)), 0.01, 0.1)
    decay_rate = jnp.clip(jnp.exp(jax.random.uniform(key_list[11], (SH,), jnp.float32, math.log(0.001953125), math.log(4.0))), 0.001953125, 4.0)
    skip_gain = jnp.clip(jax.random.uniform(key_list[12], (SH,), jnp.float32, 0.5, 1.5), 0.5, 1.5)
    prior_state = noise(part_splits[13], (REQ, SH, HP, NS), 0.3, 4.0, ((0, 4),), jnp.float32)
    return dict(queries=queries, kv_new=kv_new, page_pool=page_pool, page_owner=page_owner, page_slot=page_slot, prefix_len=prefix_len, suffix_len=suffix_len, ssm_in=ssm_in, b_in=b_in, c_in=c_in, step_size=step_size, decay_rate=decay_rate, skip_gain=skip_gain, prior_state=prior_state)


NEG = -1e+30

def reference(queries, kv_new, page_pool, page_owner, page_slot, prefix_len, suffix_len, ssm_in, b_in, c_in, step_size, decay_rate, skip_gain, prior_state):
    group = QH // KVH
    kv_half = KVH * HD
    scale = 1.0 / math.sqrt(HD)

    def one_request(packed):
        query_rows, new_rows, owners, slot_rows, prefix_limit, suffix_limit = packed
        pages = page_pool[owners[:, :, 0], slot_rows]
        prefix_rows = jnp.transpose(pages, (1, 0, 2, 3)).reshape(PREF, 2 * kv_half)
        all_rows = jnp.concatenate([prefix_rows, new_rows], axis=0)
        keys_part = all_rows[:, :kv_half].reshape(-1, KVH, HD).astype(jnp.float32)
        values_part = all_rows[:, kv_half:].reshape(-1, KVH, HD).astype(jnp.float32)
        grouped = query_rows.reshape(SUF, KVH, group, HD).astype(jnp.float32)
        scores = jnp.einsum('qhgd,khd->hgqk', grouped, keys_part, precision=lax.Precision.HIGHEST) * scale
        positions = jnp.arange(SUF, dtype=jnp.int32)
        prefix_seen = jnp.broadcast_to((jnp.arange(PREF, dtype=jnp.int32) < prefix_limit)[None, :], (SUF, PREF))
        suffix_seen = (positions[None, :] <= positions[:, None]) & (positions[None, :] < suffix_limit)
        visible = jnp.concatenate([prefix_seen, suffix_seen], axis=1)
        masked = jnp.where(visible[None, None], scores, NEG)
        biggest = lax.optimization_barrier(jnp.max(masked, axis=-1, keepdims=True))
        weights = jnp.where(visible[None, None], jnp.exp(scores - biggest), 0.0)
        totals = lax.optimization_barrier(jnp.sum(weights, axis=-1))
        rounded = lax.optimization_barrier(weights.astype(jnp.bfloat16)).astype(jnp.float32)
        mixed = jnp.einsum('hgqk,khd->hgqd', rounded, values_part, precision=lax.Precision.HIGHEST) / totals[..., None]
        mixed = jnp.transpose(mixed, (2, 0, 1, 3)).reshape(SUF, QH * HD)
        return jnp.where((positions < suffix_limit)[:, None], mixed, 0.0).astype(jnp.bfloat16)
    attn_out = lax.map(one_request, (queries, kv_new, page_owner, page_slot, prefix_len, suffix_len))
    blocks = SUF // SUF_DEV

    def one_sequence(packed):
        inputs, b_rows, c_rows, steps_dt, start_state, suffix_limit = packed
        inputs = inputs.reshape(blocks, SUF_DEV, SH, HP)
        b_rows = b_rows.reshape(blocks, SUF_DEV, NS)
        c_rows = c_rows.reshape(blocks, SUF_DEV, NS)
        steps_dt = steps_dt.reshape(blocks, SUF_DEV, SH)
        positions = jnp.arange(SUF, dtype=jnp.int32).reshape(blocks, SUF_DEV)
        lower = jnp.arange(SUF_DEV)[:, None] >= jnp.arange(SUF_DEV)[None, :]

        def block_step(state, piece):
            block_in, block_b, block_c, block_dt, block_pos = piece
            logs = jnp.cumsum(-block_dt * decay_rate[None, :], axis=0)
            last = logs[-1]
            gram = jnp.dot(block_c, block_b.T, preferred_element_type=jnp.float32)
            exponent = jnp.where(lower[None], logs.T[:, :, None] - logs.T[:, None, :], NEG)
            mixing = gram[None] * jnp.exp(exponent) * block_dt.T[:, None, :]
            mixing = lax.optimization_barrier(mixing.astype(jnp.bfloat16)).astype(jnp.float32)
            wide_in = block_in.astype(jnp.float32)
            inner = jnp.einsum('hts,shp->thp', mixing, wide_in, precision=lax.Precision.HIGHEST)
            scaled = (jnp.exp(last[None, :] - logs) * block_dt)[:, :, None] * wide_in
            scaled = lax.optimization_barrier(scaled.astype(jnp.bfloat16)).astype(jnp.float32)
            local_state = jnp.einsum('shp,sn->hpn', scaled, block_b.astype(jnp.float32), precision=lax.Precision.HIGHEST)
            carried = jnp.exp(logs)[:, :, None] * jnp.einsum('tn,hpn->thp', block_c.astype(jnp.float32), state, precision=lax.Precision.HIGHEST)
            result = inner + carried + skip_gain[None, :, None] * wide_in
            result = jnp.where((block_pos < suffix_limit)[:, None, None], result, 0.0).astype(jnp.bfloat16)
            renewed = jnp.exp(last)[:, None, None] * state + local_state
            return (renewed, result)
        final_state, outputs = lax.scan(block_step, start_state, (inputs, b_rows, c_rows, steps_dt, positions))
        return outputs.reshape(SUF, SH * HP)
    ssm_out = lax.map(one_sequence, (ssm_in, b_in, c_in, step_size, prior_state, suffix_len))
    return (attn_out, ssm_out)
```

```python
import functools
import math

import jax
import jax.numpy as jnp
from jax import lax
from jax.experimental import pallas as pl
from jax.experimental.pallas import tpu as pltpu
from jax.sharding import PartitionSpec as P

QH = 16
KVH = 4
HD = 128
SH = 32
HP = 64
NS = 128
PAGE = 8
GROUP = QH // KVH
NEG = -1e30
F32 = jnp.float32
BF16 = jnp.bfloat16


def remote(src, dst, send_sem, recv_sem, device):
    return pltpu.make_async_remote_copy(
        src_ref=src,
        dst_ref=dst,
        send_sem=send_sem,
        recv_sem=recv_sem,
        device_id=device,
        device_id_type=pl.DeviceIdType.MESH,
    )


def nt(a, b, **kw):
    return lax.dot_general(a, b, (((1,), (1,)), ((), ())), preferred_element_type=F32, **kw)


def nn(a, b, **kw):
    return jnp.dot(a, b, preferred_element_type=F32, **kw)


def iota(shape, axis):
    return lax.broadcasted_iota(jnp.int32, shape, axis)


def kernel(
    n, nb, cap, lists,
    plen, slen, codes, q, kv, pool, x, b_t, b_rows, c_rows, dt, rate, skip, prior,
    attn_o, ssm_o,
    tiles, combs, sendbuf, recv, qbuf, kbuf, vbuf, mbuf, lbuf, accbuf, obuf,
    lx, dx, l_t, dt_t, sbuf, ybuf, hin, hout,
    ts, tr, cs, cr, ps, pr, qs, qr, ks, kr, vs, vr, os, orr, hs, hr,
):
    me = lax.axis_index("cache")
    j = lax.axis_index("blk")
    tok = x.shape[0]
    width = GROUP * HD
    prefix_limit = plen[0]
    suffix_limit = slen[0]

    def zpeer(d):
        return lax.rem(me + d, n)

    def bpeer(e):
        return lax.rem(j + e, nb)

    barrier = pltpu.get_barrier_semaphore()

    def greet_z(d, carry):
        pl.semaphore_signal(barrier, inc=1, device_id={"cache": zpeer(d)}, device_id_type=pl.DeviceIdType.MESH)
        return carry

    def greet_b(e, carry):
        pl.semaphore_signal(barrier, inc=1, device_id={"blk": bpeer(e)}, device_id_type=pl.DeviceIdType.MESH)
        return carry

    lax.fori_loop(1, n, greet_z, 0)
    lax.fori_loop(1, nb, greet_b, 0)
    pl.semaphore_wait(barrier, n - 1 + nb - 1)

    def tile_copy(e):
        return remote(codes, tiles.at[j], ts.at[e], tr.at[e], {"blk": bpeer(e)})

    def q_copy(e):
        to = bpeer(e)
        return remote(q.at[:, pl.ds(pl.multiple_of(to * width, width), width)], qbuf.at[j], qs.at[e], qr.at[e], {"blk": to})

    def k_copy(e):
        to = bpeer(e)
        return remote(kv.at[:, pl.ds(pl.multiple_of(to * HD, HD), HD)], kbuf.at[j], ks.at[e], kr.at[e], {"blk": to})

    def v_copy(e):
        to = bpeer(e)
        return remote(kv.at[:, pl.ds(pl.multiple_of(KVH * HD + to * HD, HD), HD)], vbuf.at[j], vs.at[e], vr.at[e], {"blk": to})

    def comb_copy(d):
        return remote(combs.at[0], combs.at[d], cs.at[d], cr.at[d], {"cache": zpeer(d)})

    def page_copy(d):
        return remote(sendbuf.at[d], recv.at[d], ps.at[d], pr.at[d], {"cache": zpeer(d)})

    def state_copy():
        return remote(hout, hin, hs, hr, {"blk": bpeer(1)})

    def out_copy(e):
        to = bpeer(e)
        return remote(obuf.at[to], attn_o.at[:, pl.ds(pl.multiple_of(j * width, width), width)], os.at[e], orr.at[e], {"blk": to})

    def each_b(what):
        def body(e, carry):
            what(e)
            return carry
        lax.fori_loop(1, nb, body, 0)

    def each_z(what, low=1, high=n):
        def body(d, carry):
            what(d)
            return carry
        lax.fori_loop(low, high, body, 0)

    each_b(lambda e: tile_copy(e).start())
    each_b(lambda e: (q_copy(e).start(), k_copy(e).start(), v_copy(e).start()))
    tiles[j] = codes[...]
    each_b(lambda e: tile_copy(e).wait_recv())
    combs[0] = jnp.sum(tiles[...], axis=0)
    each_z(lambda d: comb_copy(d).start())
    qbuf[j] = q[:, pl.ds(pl.multiple_of(j * width, width), width)]
    kbuf[j] = kv[:, pl.ds(pl.multiple_of(j * HD, HD), HD)]
    vbuf[j] = kv[:, pl.ds(pl.multiple_of(KVH * HD + j * HD, HD), HD)]

    lanes = combs.shape[2]
    before = jnp.where(iota((lanes, lanes), 0) < iota((lanes, lanes), 1), 1.0, 0.0).astype(BF16)

    def placing(slot, owner):
        named = combs[slot, 0:1, :] == owner + 1
        flags = jnp.broadcast_to(jnp.where(named, 1.0, 0.0), (16, lanes)).astype(BF16)
        rank = nn(flags, before)[0:1].astype(jnp.int32)
        return jnp.where((rank == iota((cap, lanes), 0)) & named, 1.0, 0.0).astype(BF16)

    def packed(slot):
        spots = pool.shape[0]
        wants = jnp.where(combs[slot, 1:2, :] == iota((spots, lanes), 0), 1.0, 0.0).astype(BF16)
        chosen = nt(placing(slot, me), wants).astype(BF16)
        return nn(chosen, pool[...]).astype(BF16)

    def answer(d):
        comb_copy(d).wait_recv()
        back = n - d
        sendbuf[back] = packed(d)
        page_copy(back).start()

    each_z(answer)
    recv[0] = packed(0)

    tri = jnp.where(iota((tok, tok), 0) >= iota((tok, tok), 1), 1.0, 0.0)
    exact = dict(precision=lax.Precision.HIGHEST)
    spread = jnp.where(iota((SH, SH * HP), 0) == iota((SH, SH * HP), 1) // HP, 1.0, 0.0)
    logs = nn(tri, dt[...] * (-rate[...]), **exact)
    lx[...] = nn(logs, spread, **exact)
    dx[...] = nn(dt[...], spread, **exact)
    l_t[...] = logs.T
    dt_t[...] = dt[...].T
    gram = nt(c_rows[...], b_rows[...])
    lower = iota((tok, tok), 0) >= iota((tok, tok), 1)
    first_half = iota((tok, 2 * HP), 1) < HP

    def pair_local(pair, carry):
        at = pl.ds(pl.multiple_of(pair * 2 * HP, 2 * HP), 2 * HP)
        xs = x[:, at]
        xf = xs.astype(F32)
        ltile = lx[:, at]

        def mixed(which):
            column = ltile[:, which * HP : which * HP + 1]
            row = l_t[pl.ds(2 * pair + which, 1), :]
            step = dt_t[pl.ds(2 * pair + which, 1), :]
            decay = jnp.exp(jnp.where(lower, column - row, NEG))
            return nn((gram * decay * step).astype(BF16), xs)

        ybuf[:, at] = jnp.where(first_half, mixed(0), mixed(1)) + skip[:, at] * xf
        scaled = (jnp.exp(ltile[tok - 1 : tok] - ltile) * dx[:, at] * xf).astype(BF16)
        sbuf[:, at] = nn(b_t[...], scaled)
        return carry

    lax.fori_loop(0, SH // 2, pair_local, 0)

    def chain():
        @pl.when(j == 0)
        def _():
            def fill(pair, carry):
                at = pl.ds(pl.multiple_of(pair * 2 * HP, 2 * HP), 2 * HP)
                hin[:, at] = prior[at, :].T.astype(BF16)
                return carry
            lax.fori_loop(0, SH // 2, fill, 0)

        @pl.when(j > 0)
        def _():
            state_copy().wait_recv()

        def onward(pair, carry):
            at = pl.ds(pl.multiple_of(pair * 2 * HP, 2 * HP), 2 * HP)
            decay = jnp.exp(lx[tok - 1 : tok, at])
            hout[:, at] = (decay * hin[:, at].astype(F32) + sbuf[:, at]).astype(BF16)
            return carry

        @pl.when(j < nb - 1)
        def _():
            lax.fori_loop(0, SH // 2, onward, 0)
            state_copy().start()

        alive = j * tok + iota((tok, 2 * HP), 0) < suffix_limit

        def read(pair, carry):
            at = pl.ds(pl.multiple_of(pair * 2 * HP, 2 * HP), 2 * HP)
            total = ybuf[:, at] + jnp.exp(lx[:, at]) * nn(c_rows[...], hin[:, at])
            ssm_o[:, at] = jnp.where(alive, total, 0.0).astype(BF16)
            return carry

        lax.fori_loop(0, SH // 2, read, 0)

    scale = 1.0 / math.sqrt(HD)
    rows = GROUP * tok

    def attend(b, keys, values, seen, first=False, last=False):
        qb = jnp.concatenate([qbuf[b, :, h * HD : (h + 1) * HD] for h in range(GROUP)], axis=0)
        scores = jnp.where(seen, nt(qb, keys) * scale, NEG)
        top = jnp.max(scores, axis=1, keepdims=True)
        if not first:
            old = mbuf[b]
            top = jnp.maximum(top, old)
            factor = jnp.exp(old - top)
        weights = jnp.exp(scores - top)
        total = jnp.sum(weights, axis=1, keepdims=True)
        mixed = nn(weights.astype(BF16), values)
        if not first:
            total = total + lbuf[b] * factor
            mixed = mixed + accbuf[b] * factor
        if not last:
            mbuf[b] = top
            lbuf[b] = total
            accbuf[b] = mixed
            return None
        alive = b * tok + lax.rem(iota((rows, HD), 0), tok) < suffix_limit
        return jnp.where(alive, mixed / total, 0.0).astype(BF16)

    each_b(lambda e: (q_copy(e).wait_recv(), k_copy(e).wait_recv(), v_copy(e).wait_recv()))

    def suffix_phase():
        keys = kbuf[...].reshape(nb * tok, HD)
        values = vbuf[...].reshape(nb * tok, HD)

        def block(b, carry):
            where_q = b * tok + lax.rem(iota((rows, nb * tok), 0), tok)
            where_k = iota((rows, nb * tok), 1)
            attend(b, keys, values, (where_k <= where_q) & (where_k < suffix_limit), first=True)
            return carry

        lax.fori_loop(0, nb, block, 0)

    per = max(1, n // 4)
    groups = n // per
    order = [0, 1, 3, 2] if groups == 4 else list(range(groups))

    def page_phase(g, last):
        if g == 0:
            each_z(lambda d: page_copy(d).wait_recv(), 1, per)
        else:
            each_z(lambda d: page_copy(d).wait_recv(), g * per, (g + 1) * per)
        span = per * cap
        slots = [lax.rem(me - d + n, n) for d in range(g * per, (g + 1) * per)]
        place = jnp.concatenate([placing(0, o) for o in slots], axis=0)
        k = iota((16, lanes), 1)
        number = lax.rem(k, lists) * nb + k // lists + 1
        page = nt(number.astype(F32).astype(BF16), jnp.concatenate([place] * PAGE, axis=0))[0:1].astype(jnp.int32)
        offset = iota((1, PAGE * span), 1) // span
        seen = (page > 0) & ((page - 1) * PAGE + offset < prefix_limit)

        def part(low):
            return jnp.concatenate(
                [
                    recv[g * per : (g + 1) * per, :, low + i * HD : low + (i + 1) * HD].reshape(span, HD)
                    for i in range(PAGE)
                ],
                axis=0,
            )

        keys = part(0)
        values = part(PAGE * HD)

        def block(e, carry):
            b = bpeer(e)
            out = attend(b, keys, values, seen, last=last)
            if last:
                for h in range(GROUP):
                    obuf[b, :, h * HD : (h + 1) * HD] = out[h * tok : (h + 1) * tok]

                @pl.when(e < nb)
                def _():
                    out_copy(e).start()
            return carry

        lax.fori_loop(1, nb + 1, block, 0)

    for phase in range(groups + 1):
        if phase < nb:
            pl.when(j == phase)(chain)
        if phase == 0:
            suffix_phase()
        else:
            page_phase(order[phase - 1], phase == groups)
    attn_o[:, pl.ds(pl.multiple_of(j * width, width), width)] = obuf[j]

    each_b(lambda e: out_copy(e).wait())
    each_b(lambda e: (tile_copy(e).wait_send(), q_copy(e).wait_send(), k_copy(e).wait_send(), v_copy(e).wait_send()))
    each_z(lambda d: (comb_copy(d).wait_send(), page_copy(d).wait_send()))

    @pl.when(j < nb - 1)
    def _():
        state_copy().wait_send()


def local(
    queries, kv_new, page_pool, page_owner, page_slot, prefix_len, suffix_len,
    ssm_in, b_in, c_in, step_size, decay_rate, skip_gain, prior_state,
):
    n = lax.axis_size("cache")
    nb = lax.axis_size("blk")
    j = lax.axis_index("blk")
    tok = queries.shape[1]
    lists = page_owner.shape[2]
    lanes = nb * lists
    cap = max(16, max(2, 2 * lists // n) * nb)
    half = KVH * HD
    pages = page_pool[0]
    spots = pages.shape[0]
    chosen = jnp.stack(
        [
            lax.dynamic_slice_in_dim(pages, j * HD, HD, 2),
            lax.dynamic_slice_in_dim(pages, half + j * HD, HD, 2),
        ],
        axis=1,
    ).reshape(spots, 2 * PAGE * HD)
    if spots < 128:
        chosen = jnp.pad(chosen, ((0, 128 - spots), (0, 0)))
    pair = jnp.stack([page_owner[0, 0, :, 0] + 1, page_slot[0, 0]])
    mine = jnp.arange(lanes, dtype=jnp.int32) // lists == j
    codes = jnp.where(mine[None], jnp.tile(pair, (1, nb)), 0)
    codes = jnp.pad(codes, ((0, 6), (0, 0)))
    vmem = pl.BlockSpec(memory_space=pltpu.VMEM)
    smem = pl.BlockSpec(memory_space=pltpu.SMEM)
    dma = pltpu.SemaphoreType.DMA
    wide = SH * HP
    rows = GROUP * tok
    attn, ssm = pl.pallas_call(
        functools.partial(kernel, n, nb, cap, lists),
        out_shape=(
            jax.ShapeDtypeStruct((tok, QH * HD), BF16),
            jax.ShapeDtypeStruct((tok, wide), BF16),
        ),
        in_specs=[smem, smem] + [vmem] * 12,
        out_specs=(vmem, vmem),
        scratch_shapes=[
            pltpu.VMEM((nb, 8, lanes), jnp.int32),
            pltpu.VMEM((n, 8, lanes), jnp.int32),
            pltpu.VMEM((n, cap, 2 * PAGE * HD), BF16),
            pltpu.VMEM((n, cap, 2 * PAGE * HD), BF16),
            pltpu.VMEM((nb, tok, GROUP * HD), BF16),
            pltpu.VMEM((nb, tok, HD), BF16),
            pltpu.VMEM((nb, tok, HD), BF16),
            pltpu.VMEM((nb, rows, 1), F32),
            pltpu.VMEM((nb, rows, 1), F32),
            pltpu.VMEM((nb, rows, HD), F32),
            pltpu.VMEM((nb, tok, GROUP * HD), BF16),
            pltpu.VMEM((tok, wide), F32),
            pltpu.VMEM((tok, wide), F32),
            pltpu.VMEM((SH, tok), F32),
            pltpu.VMEM((SH, tok), F32),
            pltpu.VMEM((NS, wide), F32),
            pltpu.VMEM((tok, wide), F32),
            pltpu.VMEM((NS, wide), BF16),
            pltpu.VMEM((NS, wide), BF16),
            dma((nb,)), dma((nb,)), dma((n,)), dma((n,)), dma((n,)), dma((n,)),
            dma((nb,)), dma((nb,)), dma((nb,)), dma((nb,)), dma((nb,)), dma((nb,)),
            dma((nb,)), dma((nb,)), dma, dma,
        ],
        compiler_params=pltpu.CompilerParams(
            collective_id=0, has_side_effects=True, vmem_limit_bytes=56 * 1024 * 1024
        ),
    )(
        prefix_len, suffix_len, codes, queries[0], kv_new[0], chosen, ssm_in[0],
        b_in[0].T, b_in[0], c_in[0], step_size[0], decay_rate[None, :],
        jnp.repeat(skip_gain, HP)[None, :], prior_state[0].reshape(wide, NS),
    )
    return attn[None], ssm[None]


def solution(mesh):
    in_specs = (
        P(("groups", "cache"), "blk", None),
        P(("groups", "cache"), "blk", None),
        P(("groups", "cache"), None, None, None),
        P(("groups", "cache"), "blk", None, None),
        P(("groups", "cache"), "blk", None),
        P(("groups", "cache")),
        P(("groups", "cache")),
        P(("groups", "cache"), "blk", None),
        P(("groups", "cache"), "blk", None),
        P(("groups", "cache"), "blk", None),
        P(("groups", "cache"), "blk", None),
        P(),
        P(),
        P(("groups", "cache"), None, None, None),
    )
    out_specs = (P(("groups", "cache"), "blk", None), P(("groups", "cache"), "blk", None))
    return jax.shard_map(local, mesh=mesh, in_specs=in_specs, out_specs=out_specs, check_vma=False)
```

```python
import functools
import math

import jax
import jax.numpy as jnp
from jax import lax
from jax.experimental import pallas as pl
from jax.experimental.pallas import tpu as pltpu
from jax.sharding import PartitionSpec as P

QH = 16
KVH = 4
HD = 128
SH = 32
HP = 64
NS = 128
PAGE = 8
GROUP = QH // KVH
NEG = -1e30
F32 = jnp.float32
BF16 = jnp.bfloat16


def remote(src, dst, send_sem, recv_sem, device):
    return pltpu.make_async_remote_copy(
        src_ref=src,
        dst_ref=dst,
        send_sem=send_sem,
        recv_sem=recv_sem,
        device_id=device,
        device_id_type=pl.DeviceIdType.MESH,
    )


def nt(a, b, **kw):
    return lax.dot_general(a, b, (((1,), (1,)), ((), ())), preferred_element_type=F32, **kw)


def nn(a, b, **kw):
    return jnp.dot(a, b, preferred_element_type=F32, **kw)


def iota(shape, axis):
    return lax.broadcasted_iota(jnp.int32, shape, axis)


def kernel(
    n, nb, cap, lists,
    plen, slen, owner, slot_row, q, kv, pages, x, b_rows, c_rows, step_t, rate, gain, prior_hbm,
    attn_o, ssm_o,
    codes, pool, page_k, page_v, flat, prior, b_t, skip, load_sem,
    tiles, combs, sendbuf, recv, qbuf, kbuf, vbuf, mbuf, lbuf, accbuf, obuf,
    lx, dx, l_t, sbuf, ybuf, hin, hout,
    ts, tr, cs, cr, ps, pr, qs, qr, ks, kr, vs, vr, os, orr, hs, hr,
):
    me = lax.axis_index("cache")
    j = lax.axis_index("blk")
    tok = x.shape[0]
    width = GROUP * HD
    prefix_limit = plen[0]
    suffix_limit = slen[0]

    half = KVH * HD
    key_load = pltpu.make_async_copy(pages.at[:, :, pl.ds(pl.multiple_of(j * HD, HD), HD)], page_k, load_sem.at[0])
    value_load = pltpu.make_async_copy(pages.at[:, :, pl.ds(pl.multiple_of(half + j * HD, HD), HD)], page_v, load_sem.at[1])
    prior_load = pltpu.make_async_copy(prior_hbm, prior, load_sem.at[2])
    own_q = pltpu.make_async_copy(q.at[:, pl.ds(pl.multiple_of(j * width, width), width)], qbuf.at[j], load_sem.at[3])
    own_k = pltpu.make_async_copy(kv.at[:, pl.ds(pl.multiple_of(j * HD, HD), HD)], kbuf.at[j], load_sem.at[4])
    own_v = pltpu.make_async_copy(kv.at[:, pl.ds(pl.multiple_of(half + j * HD, HD), HD)], vbuf.at[j], load_sem.at[5])
    for load in (key_load, value_load, prior_load, own_q, own_k, own_v):
        load.start()

    def zpeer(d):
        return lax.rem(me + d, n)

    def bpeer(e):
        return lax.rem(j + e, nb)

    barrier = pltpu.get_barrier_semaphore()

    def greet_z(d, carry):
        pl.semaphore_signal(barrier, inc=1, device_id={"cache": zpeer(d)}, device_id_type=pl.DeviceIdType.MESH)
        return carry

    def greet_b(e, carry):
        pl.semaphore_signal(barrier, inc=1, device_id={"blk": bpeer(e)}, device_id_type=pl.DeviceIdType.MESH)
        return carry

    lax.fori_loop(1, n, greet_z, 0)
    lax.fori_loop(1, nb, greet_b, 0)
    line = iota((16, lists), 0)
    listed = jnp.where(line == 0, owner[...] + 1, jnp.where(line == 1, slot_row[...], 0))
    lanes = nb * lists
    spot = jnp.where(iota((lists, lanes), 0) + j * lists == iota((lists, lanes), 1), 1.0, 0.0)
    codes[...] = nn(listed.astype(F32).astype(BF16), spot.astype(BF16))[0:8].astype(jnp.int32)
    pl.semaphore_wait(barrier, n - 1 + nb - 1)

    def tile_copy(e):
        return remote(codes, tiles.at[j], ts.at[e], tr.at[e], {"blk": bpeer(e)})

    def q_copy(e):
        to = bpeer(e)
        return remote(q.at[:, pl.ds(pl.multiple_of(to * width, width), width)], qbuf.at[j], qs.at[e], qr.at[e], {"blk": to})

    def k_copy(e):
        to = bpeer(e)
        return remote(kv.at[:, pl.ds(pl.multiple_of(to * HD, HD), HD)], kbuf.at[j], ks.at[e], kr.at[e], {"blk": to})

    def v_copy(e):
        to = bpeer(e)
        return remote(kv.at[:, pl.ds(pl.multiple_of(KVH * HD + to * HD, HD), HD)], vbuf.at[j], vs.at[e], vr.at[e], {"blk": to})

    def comb_copy(d):
        return remote(combs.at[0], combs.at[d], cs.at[d], cr.at[d], {"cache": zpeer(d)})

    def page_copy(d):
        return remote(sendbuf.at[d], recv.at[d], ps.at[d], pr.at[d], {"cache": zpeer(d)})

    def state_copy():
        return remote(hout, hin, hs, hr, {"blk": bpeer(1)})

    def out_copy(e):
        to = bpeer(e)
        return remote(obuf.at[to], attn_o.at[:, pl.ds(pl.multiple_of(j * width, width), width)], os.at[e], orr.at[e], {"blk": to})

    def each_b(what):
        def body(e, carry):
            what(e)
            return carry
        lax.fori_loop(1, nb, body, 0)

    def each_z(what, low=1, high=n):
        def body(d, carry):
            what(d)
            return carry
        lax.fori_loop(low, high, body, 0)

    each_b(lambda e: tile_copy(e).start())
    each_b(lambda e: (q_copy(e).start(), k_copy(e).start(), v_copy(e).start()))
    tiles[j] = codes[...]
    spots = page_k.shape[0]
    if spots < pool.shape[0]:
        flat[...] = jnp.zeros_like(flat)
    for which, load, held in ((0, key_load, page_k), (1, value_load, page_v)):
        load.wait()
        flat[0 : spots * PAGE] = held[...].astype(F32).reshape(spots * PAGE, HD)
        for i in range(PAGE):
            at = (which * PAGE + i) * HD
            pool[:, at : at + HD] = flat[pl.ds(i, pool.shape[0], stride=PAGE), :].astype(BF16)
    each_b(lambda e: tile_copy(e).wait_recv())
    combs[0] = jnp.sum(tiles[...], axis=0)
    each_z(lambda d: comb_copy(d).start())
    before = jnp.where(iota((lanes, lanes), 0) < iota((lanes, lanes), 1), 1.0, 0.0).astype(BF16)

    def placing(slot, owner):
        named = combs[slot, 0:1, :] == owner + 1
        flags = jnp.broadcast_to(jnp.where(named, 1.0, 0.0), (16, lanes)).astype(BF16)
        rank = nn(flags, before)[0:1].astype(jnp.int32)
        return jnp.where((rank == iota((cap, lanes), 0)) & named, 1.0, 0.0).astype(BF16)

    def packed(slot):
        spots = pool.shape[0]
        wants = jnp.where(combs[slot, 1:2, :] == iota((spots, lanes), 0), 1.0, 0.0).astype(BF16)
        chosen = nt(placing(slot, me), wants).astype(BF16)
        return nn(chosen, pool[...]).astype(BF16)

    def answer(d):
        comb_copy(d).wait_recv()
        back = n - d
        sendbuf[back] = packed(d)
        page_copy(back).start()

    each_z(answer)
    recv[0] = packed(0)

    tri = jnp.where(iota((tok, tok), 0) >= iota((tok, tok), 1), 1.0, 0.0)
    exact = dict(precision=lax.Precision.HIGHEST)
    spread = jnp.where(iota((SH, SH * HP), 0) == iota((SH, SH * HP), 1) // HP, 1.0, 0.0)
    dt = step_t[...].T
    logs = nn(tri, dt * (-rate[...]), **exact)
    lx[...] = nn(logs, spread, **exact)
    dx[...] = nn(dt, spread, **exact)
    skip[...] = nn(jnp.broadcast_to(gain[...], (8, SH)), spread, **exact)
    l_t[...] = logs.T
    b_t[...] = b_rows[...].astype(F32).T.astype(BF16)
    gram = nt(c_rows[...], b_rows[...])
    lower = iota((tok, tok), 0) >= iota((tok, tok), 1)
    first_half = iota((tok, 2 * HP), 1) < HP

    def pair_local(pair, carry):
        at = pl.ds(pl.multiple_of(pair * 2 * HP, 2 * HP), 2 * HP)
        xs = x[:, at]
        xf = xs.astype(F32)
        ltile = lx[:, at]

        def mixed(which):
            column = ltile[:, which * HP : which * HP + 1]
            row = l_t[pl.ds(2 * pair + which, 1), :]
            step = step_t[pl.ds(2 * pair + which, 1), :]
            decay = jnp.exp(jnp.where(lower, column - row, NEG))
            return nn((gram * decay * step).astype(BF16), xs)

        ybuf[:, at] = jnp.where(first_half, mixed(0), mixed(1)) + skip[0:1, at] * xf
        scaled = (jnp.exp(ltile[tok - 1 : tok] - ltile) * dx[:, at] * xf).astype(BF16)
        sbuf[:, at] = nn(b_t[...], scaled)
        return carry

    lax.fori_loop(0, SH // 2, pair_local, 0)

    prior_load.wait()

    def chain():
        @pl.when(j == 0)
        def _():
            def fill(pair, carry):
                at = pl.ds(pl.multiple_of(pair * 2 * HP, 2 * HP), 2 * HP)
                hin[:, at] = prior[at, :].T.astype(BF16)
                return carry
            lax.fori_loop(0, SH // 2, fill, 0)

        @pl.when(j > 0)
        def _():
            state_copy().wait_recv()

        def onward(pair, carry):
            at = pl.ds(pl.multiple_of(pair * 2 * HP, 2 * HP), 2 * HP)
            decay = jnp.exp(lx[tok - 1 : tok, at])
            hout[:, at] = (decay * hin[:, at].astype(F32) + sbuf[:, at]).astype(BF16)
            return carry

        @pl.when(j < nb - 1)
        def _():
            lax.fori_loop(0, SH // 2, onward, 0)
            state_copy().start()

        alive = j * tok + iota((tok, 2 * HP), 0) < suffix_limit

        def read(pair, carry):
            at = pl.ds(pl.multiple_of(pair * 2 * HP, 2 * HP), 2 * HP)
            total = ybuf[:, at] + jnp.exp(lx[:, at]) * nn(c_rows[...], hin[:, at])
            ssm_o[:, at] = jnp.where(alive, total, 0.0).astype(BF16)
            return carry

        lax.fori_loop(0, SH // 2, read, 0)

    scale = math.log2(math.e) / math.sqrt(HD)
    rows = GROUP * tok

    def attend(b, keys, values_t, bias, first=False, last=False):
        qb = jnp.concatenate([qbuf[b, :, h * HD : (h + 1) * HD] for h in range(GROUP)], axis=0)
        scores = nt(keys, qb) * scale + jnp.concatenate([bias] * GROUP, axis=1)
        top = jnp.max(scores, axis=0, keepdims=True)
        if not first:
            old = mbuf[b]
            top = jnp.maximum(top, old)
            factor = jnp.exp2(old - top)
        weights = jnp.exp2(scores - top)
        total = jnp.sum(weights, axis=0, keepdims=True)
        mixed = nn(values_t, weights.astype(BF16))
        if not first:
            total = total + lbuf[b] * factor
            mixed = mixed + accbuf[b] * factor
        if not last:
            mbuf[b] = top
            lbuf[b] = total
            accbuf[b] = mixed
            return None
        return mixed * (1.0 / total)

    for load in (own_q, own_k, own_v):
        load.wait()
    each_b(lambda e: (q_copy(e).wait_recv(), k_copy(e).wait_recv(), v_copy(e).wait_recv()))

    def suffix_phase():
        keys = kbuf[...].reshape(nb * tok, HD)
        values_t = vbuf[...].reshape(nb * tok, HD).astype(F32).T.astype(BF16)

        def block(b, carry):
            where_q = b * tok + iota((nb * tok, tok), 1)
            where_k = iota((nb * tok, tok), 0)
            seen = (where_k <= where_q) & (where_k < suffix_limit)
            attend(b, keys, values_t, jnp.where(seen, 0.0, NEG), first=True)
            return carry

        lax.fori_loop(0, nb, block, 0)

    per = max(1, n // 4)
    groups = n // per
    order = [0, 1, 3, 2] if groups == 4 else list(range(groups))

    def page_phase(g, last):
        if g == 0:
            each_z(lambda d: page_copy(d).wait_recv(), 1, per)
        else:
            each_z(lambda d: page_copy(d).wait_recv(), g * per, (g + 1) * per)
        span = per * cap
        slots = [lax.rem(me - d + n, n) for d in range(g * per, (g + 1) * per)]
        place = jnp.concatenate([placing(0, o) for o in slots], axis=0)
        k = iota((lanes, tok), 0)
        number = lax.rem(k, lists) * nb + k // lists + 1
        page = nn(jnp.concatenate([place] * PAGE, axis=0), number.astype(F32).astype(BF16)).astype(jnp.int32)
        offset = jnp.concatenate([jnp.full((span, tok), i, jnp.int32) for i in range(PAGE)], axis=0)
        seen = (page > 0) & ((page - 1) * PAGE + offset < prefix_limit)
        bias = jnp.where(seen, 0.0, NEG)

        def part(low):
            return jnp.concatenate(
                [
                    recv[g * per : (g + 1) * per, :, low + i * HD : low + (i + 1) * HD].reshape(span, HD)
                    for i in range(PAGE)
                ],
                axis=0,
            )

        keys = part(0)
        values_t = part(PAGE * HD).astype(F32).T.astype(BF16)

        def block(e, carry):
            b = bpeer(e)
            out = attend(b, keys, values_t, bias, last=last)
            if last:
                alive = b * tok + iota((tok, HD), 0) < suffix_limit
                for h in range(GROUP):
                    head = out[:, h * tok : (h + 1) * tok].T
                    obuf[b, :, h * HD : (h + 1) * HD] = jnp.where(alive, head, 0.0).astype(BF16)

                @pl.when(e < nb)
                def _():
                    out_copy(e).start()
            return carry

        lax.fori_loop(1, nb + 1, block, 0)

    for phase in range(groups + 1):
        if phase < nb:
            pl.when(j == phase)(chain)
        if phase == 0:
            suffix_phase()
        else:
            page_phase(order[phase - 1], phase == groups)
    attn_o[:, pl.ds(pl.multiple_of(j * width, width), width)] = obuf[j]

    each_b(lambda e: out_copy(e).wait())
    each_b(lambda e: (tile_copy(e).wait_send(), q_copy(e).wait_send(), k_copy(e).wait_send(), v_copy(e).wait_send()))
    each_z(lambda d: (comb_copy(d).wait_send(), page_copy(d).wait_send()))

    @pl.when(j < nb - 1)
    def _():
        state_copy().wait_send()


def handed_on(attn, ssm, attn_out, ssm_out, sem):
    first = pltpu.make_async_copy(attn, attn_out, sem.at[0])
    second = pltpu.make_async_copy(ssm, ssm_out, sem.at[1])
    first.start()
    second.start()
    first.wait()
    second.wait()


def local(
    queries, kv_new, page_pool, page_owner, page_slot, prefix_len, suffix_len,
    ssm_in, b_in, c_in, step_size, decay_rate, skip_gain, prior_state,
):
    n = lax.axis_size("cache")
    nb = lax.axis_size("blk")
    tok = queries.shape[1]
    lists = page_owner.shape[2]
    lanes = nb * lists
    cap = max(16, max(2, 2 * lists // n) * nb)
    spots = page_pool.shape[1]
    deep = max(128, spots)
    vmem = pl.BlockSpec(memory_space=pltpu.VMEM)
    hbm = pl.BlockSpec(memory_space=pl.ANY)
    smem = pl.BlockSpec(memory_space=pltpu.SMEM)
    dma = pltpu.SemaphoreType.DMA
    wide = SH * HP
    rows = GROUP * tok
    attn, ssm = pl.pallas_call(
        functools.partial(kernel, n, nb, cap, lists),
        out_shape=(
            jax.ShapeDtypeStruct((tok, QH * HD), BF16),
            jax.ShapeDtypeStruct((tok, wide), BF16),
        ),
        in_specs=[smem, smem, vmem, vmem, hbm, hbm, hbm] + [vmem] * 6 + [hbm],
        out_specs=(vmem, vmem),
        scratch_shapes=[
            pltpu.VMEM((8, lanes), jnp.int32),
            pltpu.VMEM((deep, 2 * PAGE * HD), BF16),
            pltpu.VMEM((spots, PAGE, HD), BF16),
            pltpu.VMEM((spots, PAGE, HD), BF16),
            pltpu.VMEM((deep * PAGE, HD), F32),
            pltpu.VMEM((wide, NS), F32),
            pltpu.VMEM((NS, tok), BF16),
            pltpu.VMEM((8, wide), F32),
            dma((6,)),
            pltpu.VMEM((nb, 8, lanes), jnp.int32),
            pltpu.VMEM((n, 8, lanes), jnp.int32),
            pltpu.VMEM((n, cap, 2 * PAGE * HD), BF16),
            pltpu.VMEM((n, cap, 2 * PAGE * HD), BF16),
            pltpu.VMEM((nb, tok, GROUP * HD), BF16),
            pltpu.VMEM((nb, tok, HD), BF16),
            pltpu.VMEM((nb, tok, HD), BF16),
            pltpu.VMEM((nb, 1, rows), F32),
            pltpu.VMEM((nb, 1, rows), F32),
            pltpu.VMEM((nb, HD, rows), F32),
            pltpu.VMEM((nb, tok, GROUP * HD), BF16),
            pltpu.VMEM((tok, wide), F32),
            pltpu.VMEM((tok, wide), F32),
            pltpu.VMEM((SH, tok), F32),
            pltpu.VMEM((NS, wide), F32),
            pltpu.VMEM((tok, wide), F32),
            pltpu.VMEM((NS, wide), BF16),
            pltpu.VMEM((NS, wide), BF16),
            dma((nb,)), dma((nb,)), dma((n,)), dma((n,)), dma((n,)), dma((n,)),
            dma((nb,)), dma((nb,)), dma((nb,)), dma((nb,)), dma((nb,)), dma((nb,)),
            dma((nb,)), dma((nb,)), dma, dma,
        ],
        compiler_params=pltpu.CompilerParams(
            collective_id=0, has_side_effects=True, vmem_limit_bytes=56 * 1024 * 1024
        ),
    )(
        prefix_len, suffix_len, page_owner.reshape(1, lists), page_slot.reshape(1, lists),
        queries[0], kv_new[0], page_pool[0], ssm_in[0], b_in[0], c_in[0], step_size[0].T,
        decay_rate[None, :], skip_gain[None, :], prior_state[0].reshape(wide, NS),
    )
    attn, ssm = pl.pallas_call(
        handed_on,
        out_shape=(
            jax.ShapeDtypeStruct(attn.shape, BF16),
            jax.ShapeDtypeStruct(ssm.shape, BF16),
        ),
        in_specs=[hbm, hbm],
        out_specs=(hbm, hbm),
        scratch_shapes=[dma((2,))],
    )(attn, ssm)
    return attn[None], ssm[None]


def solution(mesh):
    in_specs = (
        P(("groups", "cache"), "blk", None),
        P(("groups", "cache"), "blk", None),
        P(("groups", "cache"), None, None, None),
        P(("groups", "cache"), "blk", None, None),
        P(("groups", "cache"), "blk", None),
        P(("groups", "cache")),
        P(("groups", "cache")),
        P(("groups", "cache"), "blk", None),
        P(("groups", "cache"), "blk", None),
        P(("groups", "cache"), "blk", None),
        P(("groups", "cache"), "blk", None),
        P(),
        P(),
        P(("groups", "cache"), None, None, None),
    )
    out_specs = (P(("groups", "cache"), "blk", None), P(("groups", "cache"), "blk", None))
    return jax.shard_map(local, mesh=mesh, in_specs=in_specs, out_specs=out_specs, check_vma=False)
```
